512 devices in a mesh: grow: 16 (over z), gcol: 32 (over y, x, core).
Axes of the slice: x: 4, y: 4, z: 16, core: 2. Of those that a mesh axis runs over, the one named last changes fastest.
Arguments:
- pair_elements: float32 [2048, 16384], P(('grow', 'gcol')), may hold values from -0.5 to 0.5
- valence_index: int32 [2048], P(('grow', 'gcol')), may hold values from 0 to 4095
- conduction_index: int32 [2048], P(('grow', 'gcol')), may hold values from 0 to 32767
- valence_energy: float32 [4096], replicated, may hold values from -2 to -0.25
- conduction_energy: float32 [32768], replicated, may hold values from 0.25 to 2
- chi_in: float32 [16384, 16384], P('grow', 'gcol'), may hold values from -0.75 to 0.75
Outputs:
- chi_out: float32 [16384, 16384], P('grow', 'gcol')
The draws below stay inside these ranges and needn't reach their ends.
All inputs are finite; a program needn't handle non-finite values.
Results may differ from the reference program's by a relative error of at most 0.00013.
Values sent between devices are 32-bit elements; how exact they have to be, the bound alone decides.
A program may use at most 64 MiB of HBM per device.

```python
import jax
import jax.numpy as jnp
from jax import lax

NG = 16384
NV = 4096
NC = 32768
NP = 2048


def with_ends(drawn, own_key, smallest, high):
    longest = drawn.shape.index(max(drawn.shape))
    spots = []
    for shift in (0, 1):
        where = [jax.random.randint(jax.random.fold_in(own_key, axis), (), 0, length) for axis, length in enumerate(drawn.shape)]
        where[longest] = (where[longest] + shift) % drawn.shape[longest]
        spots.append(tuple(where))
    return drawn.at[spots[0]].set(smallest).at[spots[1]].set(high)


def spiked(entries, key, source, target, blocks, factor):
    owner, partner = [(jnp.arange(entries.shape[dim]) // (entries.shape[dim] // blocks)).reshape([-1 if axis == dim else 1 for axis in range(entries.ndim)]) for dim in (source, target)]
    chosen = jax.random.permutation(key, blocks)[partner]
    strong = (owner == chosen) | (owner == (partner + blocks // 2) % blocks)
    return jnp.where(strong, factor * entries, entries)


def level_of(stream_key, shape, split, least, top_value):
    gain = 1.0
    for dim, blocks in split:
        draws = jax.random.uniform(jax.random.fold_in(jax.random.fold_in(stream_key, 6), dim), (blocks,), jnp.float32, least / len(split), top_value / len(split))
        gain = gain * jnp.repeat(jnp.exp(draws), shape[dim] // blocks).reshape((-1,) + (1,) * (len(shape) - 1 - dim))
    return gain


def centred(own_key, shape, scale, bound, cuts=(), kind=jnp.bfloat16):
    gain = level_of(own_key, shape, cuts, -0.22, 0.18) if cuts else 1.0
    array = jax.random.normal(own_key, shape, jnp.float32) * scale * gain
    return jnp.minimum(jnp.maximum(array, -bound), bound).astype(kind)


def gaussian_with(key, shape, spread, reach, split, heavy, dtype=jnp.bfloat16):
    drawn = spread * jax.random.normal(key, shape, jnp.float32)
    if split:
        drawn = drawn * level_of(key, shape, split, -0.22, 0.18)
    return jnp.clip(spiked(drawn, jax.random.fold_in(key, 3), *heavy), -reach, reach).astype(dtype)


def setup_inputs(seed: int = 0) -> dict:
    streams_of = jax.random.split(jax.random.key(seed), 7)
    pair_elements = gaussian_with(streams_of[0], (NP, NG), NP ** -0.5, 0.5, ((0, 512),), (0, 1, 512, 6.0), jnp.float32)
    valence_index = with_ends(jax.random.randint(streams_of[1], (NP,), 0, NV), jax.random.fold_in(streams_of[1], 1), 0, NV - 1).astype(jnp.int32)
    conduction_index = with_ends(jax.random.randint(streams_of[2], (NP,), 0, NC), jax.random.fold_in(streams_of[2], 1), 0, NC - 1).astype(jnp.int32)
    valence_energy = jnp.clip(jax.random.uniform(streams_of[3], (NV,), jnp.float32, -2.0, -0.25), -2.0, -0.25)
    conduction_energy = jnp.clip(jax.random.uniform(streams_of[4], (NC,), jnp.float32, 0.25, 2.0), 0.25, 2.0)
    chi_in = centred(streams_of[5], (NG, NG), 0.05, 0.75, ((0, 16), (1, 32)), jnp.float32)
    return {"pair_elements": pair_elements, "valence_index": valence_index, "conduction_index": conduction_index, "valence_energy": valence_energy, "conduction_energy": conduction_energy, "chi_in": chi_in}


def reference(pair_elements, valence_index, conduction_index, valence_energy, conduction_energy, chi_in):
    weights = 4.0 / (jnp.take(conduction_energy, conduction_index) - jnp.take(valence_energy, valence_index))
    scaled = pair_elements * weights[:, None]
    increment = lax.dot_general(scaled, pair_elements, (((0,), (0,)), ((), ())), precision=lax.Precision.HIGHEST, preferred_element_type=jnp.float32)
    return chi_in + increment
```

```python
import jax
import jax.numpy as jnp
from jax import lax
from jax.experimental import pallas as pl
from jax.experimental.pallas import tpu as pltpu
from jax.sharding import PartitionSpec as P

MESH = pl.DeviceIdType.MESH
PLANES = 16
PANELS = 32
PAIRS = 4
WIDTH = 512
SUBS = 4
DEEP = PANELS * PAIRS // SUBS
STEPS = 4 * (PLANES // 2) - 2
EDGES = (
    ((0, 0), (1, 0), (1, 2), (1, 3), (2, 0), (2, 1), (2, 2), (2, 3)),
    ((1, 0), (2, 0)),
    ((1, 1), (1, 2), (1, 3)),
    ((1, 0), (1, 3)),
)
MOVES = ((1, 0), (0, 1), (-1, 0), (0, -1))
DEEPEST = 5


def depths():
    found = {(0, 0): 0}
    for _ in range(16):
        for (da, db), nodes in zip(MOVES, EDGES):
            for a, b in nodes:
                if (a, b) in found:
                    found[((a + da) % 4, (b + db) % 4)] = found[(a, b)] + 1
    return found


DEPTHS = depths()
LAG = DEEPEST + 5


def wrap(value, size):
    return lax.rem(value + 4 * size, size)


def looked_up(table, index):
    place = lax.broadcasted_iota(jnp.int32, table.shape, 0) * 128 + lax.broadcasted_iota(
        jnp.int32, table.shape, 1
    )
    return jnp.sum(jnp.where(place == index, table, 0.0), axis=(0, 1), keepdims=True)


def split(value):
    high = value.astype(jnp.bfloat16)
    return high, (value - high.astype(jnp.float32)).astype(jnp.bfloat16)


def over_pairs(left, right):
    return lax.dot_general(
        left, right, (((0,), (0,)), ((), ())), preferred_element_type=jnp.float32
    )


def landed(ref, sem):
    pltpu.make_async_copy(ref, ref, sem).wait()


def kernel(
    valence_index, conduction_index, valence, conduction, elements, chi, out,
    outbox, inbox, cols, rows, cut,
    box_send, box_recv, ring_send, ring_recv, tree_send, tree_recv, twin_send, twin_recv, chi_sem,
):
    z = lax.axis_index("grow")
    c = lax.axis_index("gcol")
    core, x, y = lax.rem(c, 2), lax.rem(c // 2, 4), c // 8
    twin = c + 1 - 2 * core
    ahead, behind = wrap(z + 1, PLANES), wrap(z - 1, PLANES)

    barrier = pltpu.get_barrier_semaphore()

    @pl.loop(1, PANELS)
    def _(k):
        pl.semaphore_signal(
            barrier, inc=1, device_id={"gcol": wrap(c + k, PANELS)}, device_id_type=MESH
        )

    for side in (ahead, behind):
        pl.semaphore_signal(barrier, inc=1, device_id={"grow": side}, device_id_type=MESH)

    chi_copy = pltpu.make_async_copy(chi, out, chi_sem)
    chi_copy.start()

    pair = lax.broadcasted_iota(jnp.int32, (PAIRS, 1), 0)
    gaps = jnp.ones((PAIRS, 1), jnp.float32)
    for i in range(PAIRS):
        gap = looked_up(conduction[...], conduction_index[i]) - looked_up(
            valence[...], valence_index[i]
        )
        gaps = jnp.where(pair == i, gap, gaps)
    root_weights = jnp.sqrt(4.0 / gaps)
    for k in range(PANELS):
        outbox[k] = elements[:, k * WIDTH : (k + 1) * WIDTH] * root_weights

    a, b = wrap(x - lax.rem(z, 4), 4), wrap(y - z // 4, 4)
    lags, sends = [], []
    for t in range(4):
        na, nb = ((a, b), (b, -a), (-a, -b), (-b, a))[t]
        node = wrap(na, 4) * 4 + wrap(nb, 4)
        lag = jnp.int32(0)
        for (da, db), depth in DEPTHS.items():
            lag = jnp.where(node == da * 4 + db, depth, lag)
        lags.append(lag)
        row = []
        for d in range(4):
            hit = jnp.int32(0)
            for da, db in EDGES[(d - t) % 4]:
                hit = jnp.where(node == da * 4 + db, 1, hit)
            row.append(hit)
        sends.append(row)
    is_root = (a == 0) & (b == 0)
    beside = [(wrap(y + db, 4) * 4 + wrap(x + da, 4)) * 2 + core for da, db in MOVES]

    pl.semaphore_wait(barrier, PANELS + 1)

    @pl.loop(1, PANELS)
    def _(k):
        to = wrap(c + k, PANELS)
        pltpu.make_async_remote_copy(
            src_ref=outbox.at[to],
            dst_ref=inbox.at[c],
            send_sem=box_send,
            recv_sem=box_recv.at[c // 8],
            device_id={"gcol": to},
            device_id_type=MESH,
        ).start()

    pltpu.make_async_copy(outbox.at[c], inbox.at[c], box_recv.at[c // 8]).start()

    def pass_on(side, slot, step):
        pltpu.make_async_remote_copy(
            src_ref=cols.at[slot],
            dst_ref=cols.at[slot],
            send_sem=ring_send.at[side],
            recv_sem=ring_recv.at[side, step],
            device_id={"grow": (ahead, behind)[side]},
            device_id_type=MESH,
        ).start()

    for j in range(SUBS):
        landed(inbox.at[pl.ds(8 * j, 8)], box_recv.at[j])
        for k in range(8):
            cols[z * SUBS + j, k * PAIRS : (k + 1) * PAIRS, :] = inbox[8 * j + k]
        pass_on(0, z * SUBS + j, j)
        pass_on(1, z * SUBS + j, (j + 2) % 4)

    chi_copy.wait()

    @pl.loop(-SUBS, 32 + LAG)
    def _(i):
        q = wrap(i, 4)
        step = (i + 64) // 4 - 15

        def to_tree(slot):
            pltpu.make_async_copy(cols.at[slot], rows.at[core, slot], tree_recv.at[slot]).start()

        @pl.when(is_root & (i < 0))
        def _():
            to_tree(z * SUBS + q)

        @pl.when((i >= 0) & (i < STEPS))
        def _():
            for side, sub, plane in (
                (0, q, wrap(z - step, PLANES)),
                (1, wrap(q + 2, 4), wrap(z + step, PLANES)),
            ):
                slot = plane * SUBS + sub
                landed(cols.at[slot], ring_recv.at[side, i])

                @pl.when(i + SUBS < STEPS)
                def _():
                    pass_on(side, slot, i + SUBS)

                @pl.when(is_root)
                def _():
                    to_tree(slot)

        for t in range(4):
            at = i - lags[t]
            kind = wrap(at - t, 4)
            far = (at + 64) // 4 - 15
            plane = wrap(z + jnp.where(kind == 0, -far, far), PLANES)
            slot = plane * SUBS + t

            @pl.when(
                (at >= -SUBS) & (at < STEPS) & ((kind == 0) | ((kind == 2) & (at >= 0)))
            )
            def _():
                piece = rows.at[core, slot]
                landed(piece, tree_recv.at[slot])
                for d in range(4):

                    @pl.when(sends[t][d] == 1)
                    def _():
                        pltpu.make_async_remote_copy(
                            src_ref=piece,
                            dst_ref=piece,
                            send_sem=tree_send.at[t, d],
                            recv_sem=tree_recv.at[slot],
                            device_id={"gcol": beside[d]},
                            device_id_type=MESH,
                        ).start()

                pltpu.make_async_remote_copy(
                    src_ref=piece,
                    dst_ref=piece,
                    send_sem=twin_send,
                    recv_sem=twin_recv.at[slot],
                    device_id={"gcol": twin},
                    device_id_type=MESH,
                ).start()

        unit = i - LAG

        @pl.when(unit >= 0)
        def _():
            group = unit // 4
            quarter = lax.rem(unit, 4)
            planes = (
                wrap(z - jnp.where(group == 7, 0, group + 1), PLANES),
                wrap(z + group + 1, PLANES),
            )

            @pl.when(quarter == 0)
            def _():
                for h, plane in enumerate(planes):
                    for t in range(SUBS):
                        landed(rows.at[0, plane * SUBS + t], twin_recv.at[plane * SUBS + t])
                    block = cols[pl.ds(plane * SUBS, SUBS)].reshape(SUBS * DEEP, WIDTH)
                    high, low = split(block)
                    cut[0, h * 128 : (h + 1) * 128, :] = high
                    cut[1, h * 128 : (h + 1) * 128, :] = low

            half = quarter // 2
            first = pl.multiple_of(lax.rem(quarter, 2) * 256, 256)
            left = jnp.concatenate(
                [
                    rows[half, pl.ds(plane * SUBS, SUBS), :, pl.ds(first, 256)].reshape(
                        SUBS * DEEP, 256
                    )
                    for plane in planes
                ],
                axis=0,
            )
            high, low = split(left)
            place = pl.ds(pl.multiple_of(quarter * 256, 256), 256)
            out[place, :] += (
                over_pairs(high, cut[0]) + over_pairs(high, cut[1]) + over_pairs(low, cut[0])
            )

    landed(outbox.at[pl.ds(0, PANELS - 1)], box_send)
    for side in range(2):
        landed(cols.at[pl.ds(0, STEPS)], ring_send.at[side])
    for t in range(4):
        for d in range(4):

            @pl.when(sends[t][d] == 1)
            def _():
                landed(rows.at[0, pl.ds(0, PLANES)], tree_send.at[t, d])

    landed(rows.at[0], twin_send)


def per_device(
    pair_elements, valence_index, conduction_index, valence_energy, conduction_energy, chi_in
):
    slots = PLANES * SUBS
    vmem = pl.BlockSpec(memory_space=pltpu.VMEM)
    smem = pl.BlockSpec(memory_space=pltpu.SMEM)
    return pl.pallas_call(
        kernel,
        out_shape=jax.ShapeDtypeStruct(chi_in.shape, jnp.float32),
        in_specs=[smem, smem, vmem, vmem, vmem, pl.BlockSpec(memory_space=pl.ANY)],
        out_specs=vmem,
        scratch_shapes=[
            pltpu.VMEM((PANELS, PAIRS, WIDTH), jnp.float32),
            pltpu.VMEM((PANELS, PAIRS, WIDTH), jnp.float32),
            pltpu.VMEM((slots, DEEP, WIDTH), jnp.float32),
            pltpu.VMEM((2, slots, DEEP, WIDTH), jnp.float32),
            pltpu.VMEM((2, 256, WIDTH), jnp.bfloat16),
            pltpu.SemaphoreType.DMA,
            pltpu.SemaphoreType.DMA((4,)),
            pltpu.SemaphoreType.DMA((2,)),
            pltpu.SemaphoreType.DMA((2, STEPS)),
            pltpu.SemaphoreType.DMA((4, 4)),
            pltpu.SemaphoreType.DMA((slots,)),
            pltpu.SemaphoreType.DMA,
            pltpu.SemaphoreType.DMA((slots,)),
            pltpu.SemaphoreType.DMA,
        ],
        compiler_params=pltpu.CompilerParams(
            collective_id=0, has_side_effects=True, vmem_limit_bytes=40 * 1024 * 1024
        ),
    )(
        valence_index,
        conduction_index,
        valence_energy.reshape(-1, 128),
        conduction_energy.reshape(-1, 128),
        pair_elements,
        chi_in,
    )


def solution(mesh):
    placed = (
        P(("grow", "gcol"), None),
        P(("grow", "gcol")),
        P(("grow", "gcol")),
        P(),
        P(),
        P("grow", "gcol"),
    )
    return jax.shard_map(
        per_device, mesh=mesh, in_specs=placed, out_specs=P("grow", "gcol"), check_vma=False
    )
```

```python
import jax
import jax.numpy as jnp
from jax import lax
from jax.experimental import pallas as pl
from jax.experimental.pallas import tpu as pltpu
from jax.sharding import PartitionSpec as P

MESH = pl.DeviceIdType.MESH
PLANES = 16
PANELS = 32
PAIRS = 4
WIDTH = 512
SUBS = 4
DEEP = PANELS * PAIRS // SUBS
STEPS = 4 * (PLANES // 2) - 2
CHILDREN = {
    (0, 0): ((1, 0),),
    (1, 0): ((2, 0), (1, 1), (1, 3), (3, 2)),
    (2, 0): ((2, 1), (3, 0)),
    (1, 1): ((0, 1),),
    (1, 3): ((0, 3), (1, 2), (2, 3)),
    (3, 2): ((0, 2), (2, 2), (3, 1), (3, 3)),
}
PORTS = 4
FAR = (8,)
NEAR = 8 - (len(FAR) + 1) // 2
TREE_STEPS = 4 * NEAR
WAITS = (0, 4, 8, 12)
SPREAD_AT, TWIN_AT, LAY_AT = 4, 16, 24

ORDER = (0, 1, 2, 3, 7, 4, 5, 6)
START = 4 * 0 + 3 + WAITS[-1] + 2
DOUBLE = 4 * ORDER[-1] + 3 + WAITS[-1] + 2 - 4
LAST = (31 + START + DOUBLE) // 2


DEPTHS = {(0, 0): 0}
for _parent, _children in CHILDREN.items():
    for _child in _children:
        DEPTHS[_child] = DEPTHS[_parent] + 1


def wrap(value, size):
    return lax.rem(value + 4 * size, size)


def looked_up(table, index):
    place = lax.broadcasted_iota(jnp.int32, table.shape, 0) * 128 + lax.broadcasted_iota(
        jnp.int32, table.shape, 1
    )
    return jnp.sum(jnp.where(place == index, table, 0.0), axis=(0, 1), keepdims=True)


def split(value):
    high = value.astype(jnp.bfloat16)
    return high, (value - high.astype(jnp.float32)).astype(jnp.bfloat16)


def over_pairs(left, right):
    return lax.dot_general(
        left, right, (((0,), (0,)), ((), ())), preferred_element_type=jnp.float32
    )


def landed(ref, sem):
    pltpu.make_async_copy(ref, ref, sem).wait()


def kernel(
    valence_index_in, conduction_index_in, valence_in, conduction_in, elements_in, chi, out,
    valence_index, conduction_index, valence, conduction, elements,
    outbox, inbox, cols, rows, cut, far_box, spread,
    box_send, box_recv, ring_send, ring_recv, tree_send, tree_recv, twin_send, twin_recv,
    far_send, far_recv, spread_send, spread_recv, whole_send, whole_recv, in_sem,
):
    z = lax.axis_index("grow")
    c = lax.axis_index("gcol")
    core, x, y = lax.rem(c, 2), lax.rem(c // 2, 4), c // 8
    twin = c + 1 - 2 * core
    ahead, behind = wrap(z + 1, PLANES), wrap(z - 1, PLANES)

    loads = [
        pltpu.make_async_copy(source, target, in_sem.at[i])
        for i, (source, target) in enumerate(
            (
                (valence_index_in, valence_index),
                (conduction_index_in, conduction_index),
                (valence_in, valence),
                (conduction_in, conduction),
                (elements_in, elements),
                (chi, out),
            )
        )
    ]
    for load in loads:
        load.start()

    barrier = pltpu.get_barrier_semaphore()

    @pl.loop(1, PANELS)
    def _(k):
        pl.semaphore_signal(
            barrier, inc=1, device_id={"gcol": wrap(c + k, PANELS)}, device_id_type=MESH
        )

    for side in (ahead, behind, *(wrap(z + far, PLANES) for far in FAR)):
        pl.semaphore_signal(barrier, inc=1, device_id={"grow": side}, device_id_type=MESH)

    for load in loads[:5]:
        load.wait()
    pair = lax.broadcasted_iota(jnp.int32, (PAIRS, 1), 0)
    gaps = jnp.ones((PAIRS, 1), jnp.float32)
    for i in range(PAIRS):
        gap = looked_up(conduction[...], conduction_index[i]) - looked_up(
            valence[...], valence_index[i]
        )
        gaps = jnp.where(pair == i, gap, gaps)
    root_weights = jnp.sqrt(4.0 / gaps)
    for k in range(PANELS):
        outbox[k] = elements[:, k * WIDTH : (k + 1) * WIDTH] * root_weights

    a, b = wrap(x - lax.rem(z, 4), 4), wrap(y - z // 4, 4)
    lags, sends = [], []
    for t in range(4):
        na, nb = ((a, b), (b, -a), (-a, -b), (-b, a))[t]
        node = wrap(na, 4) * 4 + wrap(nb, 4)
        lag = jnp.int32(0)
        for (da, db), depth in DEPTHS.items():
            lag = jnp.where(node == da * 4 + db, WAITS[depth], lag)
        lags.append(lag)
        row = []
        for port in range(PORTS):
            hit, ca, cb = jnp.int32(0), jnp.int32(0), jnp.int32(0)
            for (da, db), children in CHILDREN.items():
                if port < len(children):
                    here = node == da * 4 + db
                    hit = jnp.where(here, 1, hit)
                    ca = jnp.where(here, children[port][0], ca)
                    cb = jnp.where(here, children[port][1], cb)
            ca, cb = ((ca, cb), (-cb, ca), (-ca, -cb), (cb, -ca))[t]
            to = (wrap(z // 4 + cb, 4) * 4 + wrap(lax.rem(z, 4) + ca, 4)) * 2 + core
            row.append((hit, to))
        sends.append(row)
    is_root = (a == 0) & (b == 0)

    pl.semaphore_wait(barrier, PANELS + 1 + len(FAR))

    for k, far in enumerate(FAR):
        to = wrap(z + far, PLANES)
        pltpu.make_async_remote_copy(
            src_ref=outbox.at[pl.ds(2 * to, 2)],
            dst_ref=far_box.at[k],
            send_sem=far_send,
            recv_sem=far_recv,
            device_id={"grow": to},
            device_id_type=MESH,
        ).start()

    @pl.loop(1, PANELS)
    def _(k):
        to = wrap(c + k, PANELS)
        pltpu.make_async_remote_copy(
            src_ref=outbox.at[to],
            dst_ref=inbox.at[c],
            send_sem=box_send,
            recv_sem=box_recv.at[c // 8],
            device_id={"gcol": to},
            device_id_type=MESH,
        ).start()

    pltpu.make_async_copy(outbox.at[c], inbox.at[c], box_recv.at[c // 8]).start()

    def pass_on(side, slot, step):
        pltpu.make_async_remote_copy(
            src_ref=cols.at[slot],
            dst_ref=cols.at[slot],
            send_sem=ring_send.at[side],
            recv_sem=ring_recv.at[side, step],
            device_id={"grow": (ahead, behind)[side]},
            device_id_type=MESH,
        ).start()

    for j in range(SUBS):
        landed(inbox.at[pl.ds(8 * j, 8)], box_recv.at[j])
        for k in range(8):
            cols[z * SUBS + j, k * PAIRS : (k + 1) * PAIRS, :] = inbox[8 * j + k]
        pass_on(0, z * SUBS + j, j)
        pass_on(1, z * SUBS + j, (j + 2) % 4)

    loads[5].wait()

    @pl.loop(-SUBS, LAST + 1)
    def _(i):
        q = wrap(i, 4)
        step = (i + 64) // 4 - 15

        def to_tree(slot):
            pltpu.make_async_copy(cols.at[slot], rows.at[core, slot], tree_recv.at[slot]).start()

        @pl.when(is_root & (i < 0))
        def _():
            to_tree(z * SUBS + q)

        @pl.when((i >= 0) & (i < STEPS))
        def _():
            for side, sub, plane in (
                (0, q, wrap(z - step, PLANES)),
                (1, wrap(q + 2, 4), wrap(z + step, PLANES)),
            ):
                slot = plane * SUBS + sub
                landed(cols.at[slot], ring_recv.at[side, i])

                @pl.when(i + SUBS < STEPS)
                def _():
                    pass_on(side, slot, i + SUBS)

                @pl.when(is_root & (i < TREE_STEPS))
                def _():
                    to_tree(slot)

        for t in range(4):
            at = i - lags[t]
            kind = wrap(at - t, 4)
            far = (at + 64) // 4 - 15
            plane = wrap(z + jnp.where(kind == 0, -far, far), PLANES)
            slot = plane * SUBS + t

            @pl.when(
                (at >= -SUBS) & (at < TREE_STEPS) & ((kind == 0) | ((kind == 2) & (at >= 0)))
            )
            def _():
                piece = rows.at[core, slot]
                landed(piece, tree_recv.at[slot])
                for d, (hit, to) in enumerate(sends[t]):

                    @pl.when(hit == 1)
                    def _():
                        pltpu.make_async_remote_copy(
                            src_ref=piece,
                            dst_ref=piece,
                            send_sem=tree_send.at[t, d],
                            recv_sem=tree_recv.at[slot],
                            device_id={"gcol": to},
                            device_id_type=MESH,
                        ).start()

                pltpu.make_async_remote_copy(
                    src_ref=piece,
                    dst_ref=piece,
                    send_sem=twin_send,
                    recv_sem=twin_recv.at[slot],
                    device_id={"gcol": twin},
                    device_id_type=MESH,
                ).start()

        line = c // 2

        @pl.when(i == SPREAD_AT)
        def _():
            landed(far_box, far_recv)
            pltpu.make_async_copy(far_box, spread.at[core, line], spread_recv).start()

            @pl.loop(1, PANELS // 2)
            def _(k):
                pltpu.make_async_remote_copy(
                    src_ref=far_box,
                    dst_ref=spread.at[core, line],
                    send_sem=spread_send,
                    recv_sem=spread_recv,
                    device_id={"gcol": wrap(c + 2 * k, PANELS)},
                    device_id_type=MESH,
                ).start()

        @pl.when(i == TWIN_AT)
        def _():
            landed(spread.at[core], spread_recv)
            pltpu.make_async_remote_copy(
                src_ref=spread.at[core],
                dst_ref=spread.at[core],
                send_sem=whole_send,
                recv_sem=whole_recv,
                device_id={"gcol": twin},
                device_id_type=MESH,
            ).start()

        @pl.when(i == LAY_AT)
        def _():
            landed(spread.at[core], whole_recv)

        for k, far in enumerate(FAR):

            @pl.when(i == LAY_AT + k // 2)
            def _():
                plane = wrap(z - far, PLANES)

                @pl.loop(0, SUBS)
                def _(j):
                    for m in range(8):
                        for half in range(2):
                            rows[half, plane * SUBS + j, m * PAIRS : (m + 1) * PAIRS, :] = spread[
                                m % 2, j * 4 + m // 2, k, half
                            ]

        @pl.loop(0, jnp.where(i < DOUBLE, 1, 2))
        def _(turn):
            unit = i - START + jnp.maximum(i - DOUBLE, 0) + turn
            quarter = lax.rem(unit + 64, 4)
            turn_of = jnp.maximum(unit, 0) // 4
            group = jnp.int32(0)
            for turn_at, one in enumerate(ORDER):
                group = jnp.where(turn_of == turn_at, one, group)
            planes = (
                wrap(z - jnp.where(group == 7, 0, group + 1), PLANES),
                wrap(z + group + 1, PLANES),
            )

            @pl.when((unit >= 0) & (unit < 32) & (quarter == 0))
            def _():
                for h, plane in enumerate(planes):
                    by_tree = (group < NEAR) if h else (group < NEAR) | (group == 7)

                    @pl.when(by_tree)
                    def _():
                        for t in range(SUBS):
                            slot = plane * SUBS + t
                            landed(rows.at[0, slot], twin_recv.at[slot])

                    block = cols[pl.ds(plane * SUBS, SUBS)].reshape(SUBS * DEEP, WIDTH)
                    high, low = split(block)
                    cut[0, h * 128 : (h + 1) * 128, :] = high
                    cut[1, h * 128 : (h + 1) * 128, :] = low

            @pl.when((unit >= 0) & (unit < 32))
            def _():
                half = quarter // 2
                first = pl.multiple_of(lax.rem(quarter, 2) * 256, 256)
                left = jnp.concatenate(
                    [
                        rows[half, pl.ds(plane * SUBS, SUBS), :, pl.ds(first, 256)].reshape(
                            SUBS * DEEP, 256
                        )
                        for plane in planes
                    ],
                    axis=0,
                )
                high, low = split(left)
                place = pl.ds(pl.multiple_of(quarter * 256, 256), 256)
                out[place, :] += (
                    over_pairs(high, cut[0]) + over_pairs(high, cut[1]) + over_pairs(low, cut[0])
                )

    landed(outbox.at[pl.ds(0, PANELS - 1)], box_send)
    for side in range(2):
        landed(cols.at[pl.ds(0, STEPS)], ring_send.at[side])
    for t in range(4):
        for d, (hit, _) in enumerate(sends[t]):

            @pl.when(hit == 1)
            def _():
                landed(rows.at[0, pl.ds(0, PLANES - len(FAR))], tree_send.at[t, d])

    landed(rows.at[0, pl.ds(0, (PLANES - len(FAR)) * SUBS)], twin_send)
    landed(far_box, far_send)
    landed(spread.at[0, pl.ds(0, PANELS // 2 - 1)], spread_send)
    landed(spread.at[core], whole_send)


def per_device(
    pair_elements, valence_index, conduction_index, valence_energy, conduction_energy, chi_in
):
    slots = PLANES * SUBS
    return pl.pallas_call(
        kernel,
        out_shape=jax.ShapeDtypeStruct(chi_in.shape, jnp.float32),
        in_specs=[pl.BlockSpec(memory_space=pltpu.HBM)] * 6,
        out_specs=pl.BlockSpec(memory_space=pltpu.VMEM),
        scratch_shapes=[
            pltpu.SMEM((PAIRS,), jnp.int32),
            pltpu.SMEM((PAIRS,), jnp.int32),
            pltpu.VMEM((valence_energy.size // 128, 128), jnp.float32),
            pltpu.VMEM((conduction_energy.size // 128, 128), jnp.float32),
            pltpu.VMEM(pair_elements.shape, jnp.float32),
            pltpu.VMEM((PANELS, PAIRS, WIDTH), jnp.float32),
            pltpu.VMEM((PANELS, PAIRS, WIDTH), jnp.float32),
            pltpu.VMEM((slots, DEEP, WIDTH), jnp.float32),
            pltpu.VMEM((2, slots, DEEP, WIDTH), jnp.float32),
            pltpu.VMEM((2, 256, WIDTH), jnp.bfloat16),
            pltpu.VMEM((len(FAR), 2, PAIRS, WIDTH), jnp.float32),
            pltpu.VMEM((2, PANELS // 2, len(FAR), 2, PAIRS, WIDTH), jnp.float32),
            pltpu.SemaphoreType.DMA,
            pltpu.SemaphoreType.DMA((4,)),
            pltpu.SemaphoreType.DMA((2,)),
            pltpu.SemaphoreType.DMA((2, STEPS)),
            pltpu.SemaphoreType.DMA((4, PORTS)),
            pltpu.SemaphoreType.DMA((slots,)),
            pltpu.SemaphoreType.DMA,
            pltpu.SemaphoreType.DMA((slots,)),
            *[pltpu.SemaphoreType.DMA] * 6,
            pltpu.SemaphoreType.DMA((6,)),
        ],
        compiler_params=pltpu.CompilerParams(
            collective_id=0, has_side_effects=True, vmem_limit_bytes=63 * 1024 * 1024
        ),
    )(
        valence_index,
        conduction_index,
        valence_energy.reshape(-1, 128),
        conduction_energy.reshape(-1, 128),
        pair_elements,
        chi_in,
    )


def solution(mesh):
    placed = (
        P(("grow", "gcol"), None),
        P(("grow", "gcol")),
        P(("grow", "gcol")),
        P(),
        P(),
        P("grow", "gcol"),
    )
    return jax.shard_map(
        per_device, mesh=mesh, in_specs=placed, out_specs=P("grow", "gcol"), check_vma=False
    )
```

```python
import jax
import jax.numpy as jnp
from jax import lax
from jax.experimental import pallas as pl
from jax.experimental.pallas import tpu as pltpu
from jax.sharding import PartitionSpec as P

MESH = pl.DeviceIdType.MESH
PLANES = 16
PANELS = 32
PAIRS = 4
WIDTH = 512
SUBS = 4
DEEP = PANELS * PAIRS // SUBS
STEPS = 4 * (PLANES // 2) - 2
BLOCKS = 4
SLOT = {**{d: 2 * d - 2 for d in range(1, 8)}, **{16 - d: 2 * d - 1 for d in range(1, 8)}, 8: 14, 0: 15}
FIRST_AT, SECOND_AT, TWIN_AT = (0, 1, 3, 5), (3, 7, 11, 15), (9, 14, 18, 22)
START, DOUBLE = 12, 20
LAST = (31 + START + DOUBLE) // 2


def wrap(value, size):
    return lax.rem(value + 4 * size, size)


def looked_up(table, index):
    place = lax.broadcasted_iota(jnp.int32, table.shape, 0) * 128 + lax.broadcasted_iota(
        jnp.int32, table.shape, 1
    )
    return jnp.sum(jnp.where(place == index, table, 0.0), axis=(0, 1), keepdims=True)


def split(value):
    high = value.astype(jnp.bfloat16)
    return high, (value - high.astype(jnp.float32)).astype(jnp.bfloat16)


def over_pairs(left, right):
    return lax.dot_general(
        left, right, (((0,), (0,)), ((), ())), preferred_element_type=jnp.float32
    )


def landed(ref, sem):
    pltpu.make_async_copy(ref, ref, sem).wait()


def kernel(
    valence_index_in, conduction_index_in, valence_in, conduction_in, elements_in, chi, out,
    valence_index, conduction_index, valence, conduction, elements,
    outbox, inbox, row_box, cols, rows, cut,
    box_send, box_recv, ring_send, ring_recv, row_send, row_recv,
    first_send, first_recv, second_send, second_recv, twin_send, twin_recv, in_sem,
):
    z = lax.axis_index("grow")
    c = lax.axis_index("gcol")
    core, x, y = lax.rem(c, 2), lax.rem(c // 2, 4), c // 8
    twin = c + 1 - 2 * core
    ahead, behind = wrap(z + 1, PLANES), wrap(z - 1, PLANES)

    loads = [
        pltpu.make_async_copy(source, target, in_sem.at[i])
        for i, (source, target) in enumerate(
            (
                (valence_index_in, valence_index),
                (conduction_index_in, conduction_index),
                (valence_in, valence),
                (conduction_in, conduction),
                (elements_in, elements),
                (chi, out),
            )
        )
    ]
    for load in loads:
        load.start()

    barrier = pltpu.get_barrier_semaphore()

    @pl.loop(1, PANELS)
    def _(k):
        pl.semaphore_signal(
            barrier, inc=1, device_id={"gcol": wrap(c + k, PANELS)}, device_id_type=MESH
        )

    @pl.loop(1, PLANES)
    def _(k):
        for half in range(2):
            pl.semaphore_signal(
                barrier,
                inc=1,
                device_id={"grow": wrap(z + k, PLANES), "gcol": c - core + half},
                device_id_type=MESH,
            )

    for load in loads[:5]:
        load.wait()
    pair = lax.broadcasted_iota(jnp.int32, (PAIRS, 1), 0)
    gaps = jnp.ones((PAIRS, 1), jnp.float32)
    for i in range(PAIRS):
        gap = looked_up(conduction[...], conduction_index[i]) - looked_up(
            valence[...], valence_index[i]
        )
        gaps = jnp.where(pair == i, gap, gaps)
    root_weights = jnp.sqrt(4.0 / gaps)
    for k in range(PANELS):
        outbox[k] = elements[:, k * WIDTH : (k + 1) * WIDTH] * root_weights

    first, second = jnp.where(core == 0, x, y), jnp.where(core == 0, y, x)

    def at(second_place, first_place):
        line = jnp.where(
            core == 0, second_place * 4 + first_place, first_place * 4 + second_place
        )
        return line * 2 + core

    pl.semaphore_wait(barrier, PANELS - 1 + 2 * (PLANES - 1))

    by_row, by_column = (y * 4 + x) * 2 + core, (x * 4 + y) * 2 + core

    @pl.loop(1, PANELS)
    def _(k):
        to = wrap(c + k, PANELS)
        place = jnp.where(lax.rem(to, 2) == 0, by_row, by_column)
        pltpu.make_async_remote_copy(
            src_ref=outbox.at[to],
            dst_ref=inbox.at[place],
            send_sem=box_send,
            recv_sem=box_recv.at[place // 8],
            device_id={"gcol": to},
            device_id_type=MESH,
        ).start()

    own = jnp.where(core == 0, by_row, by_column)
    pltpu.make_async_copy(outbox.at[c], inbox.at[own], box_recv.at[own // 8]).start()

    for distance, slot in sorted(SLOT.items(), key=lambda item: item[1]):
        to = wrap(z - distance, PLANES)
        for half in range(2):
            source, target = outbox.at[2 * to + half], row_box.at[slot, core]
            arrived = row_recv.at[slot // 4]

            def send(source=source, target=target, arrived=arrived, to=to, half=half):
                pltpu.make_async_remote_copy(
                    src_ref=source,
                    dst_ref=target,
                    send_sem=row_send,
                    recv_sem=arrived,
                    device_id={"grow": to, "gcol": c - core + half},
                    device_id_type=MESH,
                ).start()

            if distance:
                send()
            else:
                pl.when(core != half)(send)

                @pl.when(core == half)
                def _(source=source, target=target, arrived=arrived):
                    pltpu.make_async_copy(source, target, arrived).start()

    def pass_on(side, slot, step):
        pltpu.make_async_remote_copy(
            src_ref=cols.at[slot],
            dst_ref=cols.at[slot],
            send_sem=ring_send.at[side],
            recv_sem=ring_recv.at[side, step],
            device_id={"grow": (ahead, behind)[side]},
            device_id_type=MESH,
        ).start()

    for j in range(SUBS):
        landed(inbox.at[pl.ds(8 * j, 8)], box_recv.at[j])
        for k in range(8):
            cols[z * SUBS + j, k * PAIRS : (k + 1) * PAIRS, :] = inbox[8 * j + k]
        pass_on(0, z * SUBS + j, j)
        pass_on(1, z * SUBS + j, (j + 2) % 4)

    loads[5].wait()

    @pl.loop(-SUBS, LAST + 1)
    def _(i):
        q = wrap(i, 4)
        step = (i + 64) // 4 - 15

        @pl.when((i >= 0) & (i < STEPS))
        def _():
            for side, sub, plane in (
                (0, q, wrap(z - step, PLANES)),
                (1, wrap(q + 2, 4), wrap(z + step, PLANES)),
            ):
                slot = plane * SUBS + sub
                landed(cols.at[slot], ring_recv.at[side, i])

                @pl.when(i + SUBS < STEPS)
                def _():
                    pass_on(side, slot, i + SUBS)

        for block in range(BLOCKS):

            @pl.when(i == FIRST_AT[block])
            def _():
                landed(row_box.at[pl.ds(4 * block, 4)], row_recv.at[block])
                for slot in range(4):
                    for part in range(2):
                        rows[
                            core, block, second, first, slot, part * PAIRS : (part + 1) * PAIRS, :
                        ] = row_box[4 * block + slot, part]
                piece = rows.at[core, block, second, first]
                for k in range(1, 4):
                    pltpu.make_async_remote_copy(
                        src_ref=piece,
                        dst_ref=piece,
                        send_sem=first_send,
                        recv_sem=first_recv.at[block],
                        device_id={"gcol": at(second, wrap(first + k, 4))},
                        device_id_type=MESH,
                    ).start()

            @pl.when(i == SECOND_AT[block])
            def _():
                landed(rows.at[core, block, second, pl.ds(0, 3)], first_recv.at[block])
                piece = rows.at[core, block, second]
                for k in range(1, 4):
                    pltpu.make_async_remote_copy(
                        src_ref=piece,
                        dst_ref=piece,
                        send_sem=second_send,
                        recv_sem=second_recv.at[block],
                        device_id={"gcol": at(wrap(second + k, 4), first)},
                        device_id_type=MESH,
                    ).start()

            @pl.when(i == TWIN_AT[block])
            def _():
                landed(rows.at[core, block, pl.ds(0, 3)], second_recv.at[block])
                for k in range(4):
                    pltpu.make_async_remote_copy(
                        src_ref=rows.at[core, block, k],
                        dst_ref=rows.at[core, block, pl.ds(0, 4), k],
                        send_sem=twin_send,
                        recv_sem=twin_recv.at[block],
                        device_id={"gcol": twin},
                        device_id_type=MESH,
                    ).start()

        @pl.loop(0, jnp.where(i < DOUBLE, 1, 2))
        def _(turn):
            unit = i - START + jnp.maximum(i - DOUBLE, 0) + turn
            quarter = lax.rem(unit + 64, 4)
            group = jnp.maximum(unit, 0) // 4
            block = group // 2
            planes = (
                wrap(z + group + 1, PLANES),
                wrap(z - jnp.where(group == 7, 0, group + 1), PLANES),
            )

            @pl.when((unit >= 0) & (unit < 32) & (lax.rem(unit + 64, 8) == 0))
            def _():
                landed(rows.at[0, block], twin_recv.at[block])

            @pl.when((unit >= 0) & (unit < 32) & (quarter == 0))
            def _():
                for h, plane in enumerate(planes):
                    values = cols[pl.ds(plane * SUBS, SUBS)].reshape(SUBS * DEEP, WIDTH)
                    high, low = split(values)
                    cut[0, h * 128 : (h + 1) * 128, :] = high
                    cut[1, h * 128 : (h + 1) * 128, :] = low

            @pl.when((unit >= 0) & (unit < 32))
            def _():
                half = quarter // 2
                start = pl.multiple_of(lax.rem(quarter, 2) * 256, 256)
                slot = lax.rem(group, 2) * 2
                left = jnp.concatenate(
                    [
                        rows[half, block, :, :, slot + h, :, pl.ds(start, 256)].reshape(
                            SUBS * DEEP, 256
                        )
                        for h in range(2)
                    ],
                    axis=0,
                )
                high, low = split(left)
                place = pl.ds(pl.multiple_of(quarter * 256, 256), 256)
                out[place, :] += (
                    over_pairs(high, cut[0]) + over_pairs(high, cut[1]) + over_pairs(low, cut[0])
                )

    landed(outbox.at[pl.ds(0, PANELS - 1)], box_send)
    for side in range(2):
        landed(cols.at[pl.ds(0, STEPS)], ring_send.at[side])
    landed(inbox.at[pl.ds(0, 2 * PLANES - 1)], row_send)

    landed(rows.at[0, 0, pl.ds(0, 3)], first_send)
    landed(rows.at[0, pl.ds(0, 3)], second_send)
    landed(rows.at[0], twin_send)


def per_device(
    pair_elements, valence_index, conduction_index, valence_energy, conduction_energy, chi_in
):
    return pl.pallas_call(
        kernel,
        out_shape=jax.ShapeDtypeStruct(chi_in.shape, jnp.float32),
        in_specs=[pl.BlockSpec(memory_space=pltpu.HBM)] * 6,
        out_specs=pl.BlockSpec(memory_space=pltpu.VMEM),
        scratch_shapes=[
            pltpu.SMEM((PAIRS,), jnp.int32),
            pltpu.SMEM((PAIRS,), jnp.int32),
            pltpu.VMEM((valence_energy.size // 128, 128), jnp.float32),
            pltpu.VMEM((conduction_energy.size // 128, 128), jnp.float32),
            pltpu.VMEM(pair_elements.shape, jnp.float32),
            pltpu.VMEM((PANELS, PAIRS, WIDTH), jnp.float32),
            pltpu.VMEM((PANELS, PAIRS, WIDTH), jnp.float32),
            pltpu.VMEM((PLANES, 2, PAIRS, WIDTH), jnp.float32),
            pltpu.VMEM((PLANES * SUBS, DEEP, WIDTH), jnp.float32),
            pltpu.VMEM((2, BLOCKS, 4, 4, 4, 2 * PAIRS, WIDTH), jnp.float32),
            pltpu.VMEM((2, 256, WIDTH), jnp.bfloat16),
            pltpu.SemaphoreType.DMA,
            pltpu.SemaphoreType.DMA((4,)),
            pltpu.SemaphoreType.DMA((2,)),
            pltpu.SemaphoreType.DMA((2, STEPS)),
            *[pltpu.SemaphoreType.DMA, pltpu.SemaphoreType.DMA((BLOCKS,))] * 4,
            pltpu.SemaphoreType.DMA((6,)),
        ],
        compiler_params=pltpu.CompilerParams(
            collective_id=0, has_side_effects=True, vmem_limit_bytes=63 * 1024 * 1024
        ),
    )(
        valence_index,
        conduction_index,
        valence_energy.reshape(-1, 128),
        conduction_energy.reshape(-1, 128),
        pair_elements,
        chi_in,
    )


def solution(mesh):
    placed = (
        P(("grow", "gcol"), None),
        P(("grow", "gcol")),
        P(("grow", "gcol")),
        P(),
        P(),
        P("grow", "gcol"),
    )
    return jax.shard_map(
        per_device, mesh=mesh, in_specs=placed, out_specs=P("grow", "gcol"), check_vma=False
    )
```

```python
import jax
import jax.numpy as jnp
from jax import lax
from jax.experimental import pallas as pl
from jax.experimental.pallas import tpu as pltpu
from jax.sharding import PartitionSpec as P

MESH = pl.DeviceIdType.MESH
PLANES = 16
PANELS = 32
PAIRS = 4
WIDTH = 512
SUBS = 4
DEEP = PANELS * PAIRS // SUBS
STEPS = 4 * (PLANES // 2) - 2
BLOCKS = 4
SLOT = {**{d: 2 * d - 2 for d in range(1, 8)}, **{16 - d: 2 * d - 1 for d in range(1, 8)}, 8: 14, 0: 15}
SWAP_AT = (0, 2, 4, 6)
FIRST_AT, SECOND_AT, TWIN_AT = (1, 3, 5, 7), (5, 9, 13, 17), (12, 17, 21, 25)
START, DOUBLE = 15, 16
LAST = (31 + START + DOUBLE) // 2


def wrap(value, size):
    return lax.rem(value + 4 * size, size)


def looked_up(table, index):
    place = lax.broadcasted_iota(jnp.int32, table.shape, 0) * 128 + lax.broadcasted_iota(
        jnp.int32, table.shape, 1
    )
    return jnp.sum(jnp.where(place == index, table, 0.0), axis=(0, 1), keepdims=True)


def split(value):
    high = value.astype(jnp.bfloat16)
    return high, (value - high.astype(jnp.float32)).astype(jnp.bfloat16)


def over_pairs(left, right):
    return lax.dot_general(
        left, right, (((0,), (0,)), ((), ())), preferred_element_type=jnp.float32
    )


def landed(ref, sem):
    pltpu.make_async_copy(ref, ref, sem).wait()


def kernel(
    valence_index_in, conduction_index_in, valence_in, conduction_in, elements_in, chi, out,
    valence_index, conduction_index, valence, conduction, elements,
    outbox, inbox, row_box, swap_box, cols, rows, cut,
    box_send, box_recv, ring_send, ring_recv, row_send, row_recv,
    swap_send, swap_recv,
    first_send, first_recv, second_send, second_recv, twin_send, twin_recv, in_sem,
):
    z = lax.axis_index("grow")
    c = lax.axis_index("gcol")
    core, x, y = lax.rem(c, 2), lax.rem(c // 2, 4), c // 8
    twin = c + 1 - 2 * core
    ahead, behind = wrap(z + 1, PLANES), wrap(z - 1, PLANES)

    loads = [
        pltpu.make_async_copy(source, target, in_sem.at[i])
        for i, (source, target) in enumerate(
            (
                (valence_index_in, valence_index),
                (conduction_index_in, conduction_index),
                (valence_in, valence),
                (conduction_in, conduction),
                (elements_in, elements),
                (chi, out),
            )
        )
    ]
    for load in loads:
        load.start()

    barrier = pltpu.get_barrier_semaphore()

    @pl.loop(1, PANELS)
    def _(k):
        pl.semaphore_signal(
            barrier, inc=1, device_id={"gcol": wrap(c + k, PANELS)}, device_id_type=MESH
        )

    @pl.loop(1, PLANES)
    def _(k):
        pl.semaphore_signal(
            barrier, inc=1, device_id={"grow": wrap(z + k, PLANES)}, device_id_type=MESH
        )

    for load in loads[:5]:
        load.wait()
    pair = lax.broadcasted_iota(jnp.int32, (PAIRS, 1), 0)
    gaps = jnp.ones((PAIRS, 1), jnp.float32)
    for i in range(PAIRS):
        gap = looked_up(conduction[...], conduction_index[i]) - looked_up(
            valence[...], valence_index[i]
        )
        gaps = jnp.where(pair == i, gap, gaps)
    root_weights = jnp.sqrt(4.0 / gaps)
    for k in range(PANELS):
        outbox[k] = elements[:, k * WIDTH : (k + 1) * WIDTH] * root_weights

    first, second = jnp.where(core == 0, x, y), jnp.where(core == 0, y, x)

    def at(second_place, first_place):
        line = jnp.where(
            core == 0, second_place * 4 + first_place, first_place * 4 + second_place
        )
        return line * 2 + core

    pl.semaphore_wait(barrier, PANELS - 1 + PLANES - 1)

    by_row, by_column = (y * 4 + x) * 2 + core, (x * 4 + y) * 2 + core

    @pl.loop(1, PANELS)
    def _(k):
        to = wrap(c + k, PANELS)
        place = jnp.where(lax.rem(to, 2) == 0, by_row, by_column)
        pltpu.make_async_remote_copy(
            src_ref=outbox.at[to],
            dst_ref=inbox.at[place],
            send_sem=box_send,
            recv_sem=box_recv.at[place // 8],
            device_id={"gcol": to},
            device_id_type=MESH,
        ).start()

    own = jnp.where(core == 0, by_row, by_column)
    pltpu.make_async_copy(outbox.at[c], inbox.at[own], box_recv.at[own // 8]).start()

    for distance, slot in sorted(SLOT.items(), key=lambda item: item[1]):
        to = wrap(z - distance, PLANES)
        source = outbox.at[pl.ds(2 * to, 2)]
        if distance:
            pltpu.make_async_remote_copy(
                src_ref=source,
                dst_ref=row_box.at[slot],
                send_sem=row_send,
                recv_sem=row_recv.at[slot // 4],
                device_id={"grow": to},
                device_id_type=MESH,
            ).start()
        else:
            pltpu.make_async_copy(source, row_box.at[slot], row_recv.at[slot // 4]).start()

    def pass_on(side, slot, step):
        pltpu.make_async_remote_copy(
            src_ref=cols.at[slot],
            dst_ref=cols.at[slot],
            send_sem=ring_send.at[side],
            recv_sem=ring_recv.at[side, step],
            device_id={"grow": (ahead, behind)[side]},
            device_id_type=MESH,
        ).start()

    for j in range(SUBS):
        landed(inbox.at[pl.ds(8 * j, 8)], box_recv.at[j])
        for k in range(8):
            cols[z * SUBS + j, k * PAIRS : (k + 1) * PAIRS, :] = inbox[8 * j + k]
        pass_on(0, z * SUBS + j, j)
        pass_on(1, z * SUBS + j, (j + 2) % 4)

    loads[5].wait()

    @pl.loop(-SUBS, LAST + 1)
    def _(i):
        q = wrap(i, 4)
        step = (i + 64) // 4 - 15

        @pl.when((i >= 0) & (i < STEPS))
        def _():
            for side, sub, plane in (
                (0, q, wrap(z - step, PLANES)),
                (1, wrap(q + 2, 4), wrap(z + step, PLANES)),
            ):
                slot = plane * SUBS + sub
                landed(cols.at[slot], ring_recv.at[side, i])

                @pl.when(i + SUBS < STEPS)
                def _():
                    pass_on(side, slot, i + SUBS)

        for block in range(BLOCKS):

            @pl.when(i == SWAP_AT[block])
            def _():
                landed(row_box.at[pl.ds(4 * block, 4)], row_recv.at[block])
                pltpu.make_async_remote_copy(
                    src_ref=row_box.at[pl.ds(4 * block, 4), 1 - core],
                    dst_ref=swap_box.at[pl.ds(4 * block, 4)],
                    send_sem=swap_send,
                    recv_sem=swap_recv.at[block],
                    device_id={"gcol": twin},
                    device_id_type=MESH,
                ).start()

            @pl.when(i == FIRST_AT[block])
            def _():
                landed(swap_box.at[pl.ds(4 * block, 4)], swap_recv.at[block])
                for slot in range(4):
                    own = row_box[4 * block + slot, core]
                    other = swap_box[4 * block + slot]
                    rows[core, block, second, first, slot, :PAIRS, :] = jnp.where(
                        core == 0, own, other
                    )
                    rows[core, block, second, first, slot, PAIRS:, :] = jnp.where(
                        core == 0, other, own
                    )
                piece = rows.at[core, block, second, first]
                for k in range(1, 4):
                    pltpu.make_async_remote_copy(
                        src_ref=piece,
                        dst_ref=piece,
                        send_sem=first_send,
                        recv_sem=first_recv.at[block],
                        device_id={"gcol": at(second, wrap(first + k, 4))},
                        device_id_type=MESH,
                    ).start()

            @pl.when(i == SECOND_AT[block])
            def _():
                landed(rows.at[core, block, second, pl.ds(0, 3)], first_recv.at[block])
                piece = rows.at[core, block, second]
                for k in range(1, 4):
                    pltpu.make_async_remote_copy(
                        src_ref=piece,
                        dst_ref=piece,
                        send_sem=second_send,
                        recv_sem=second_recv.at[block],
                        device_id={"gcol": at(wrap(second + k, 4), first)},
                        device_id_type=MESH,
                    ).start()

            @pl.when(i == TWIN_AT[block])
            def _():
                landed(rows.at[core, block, pl.ds(0, 3)], second_recv.at[block])
                for k in range(4):
                    pltpu.make_async_remote_copy(
                        src_ref=rows.at[core, block, k],
                        dst_ref=rows.at[core, block, pl.ds(0, 4), k],
                        send_sem=twin_send,
                        recv_sem=twin_recv.at[block],
                        device_id={"gcol": twin},
                        device_id_type=MESH,
                    ).start()

        @pl.loop(0, jnp.where(i < DOUBLE, 1, 2))
        def _(turn):
            unit = i - START + jnp.maximum(i - DOUBLE, 0) + turn
            quarter = lax.rem(unit + 64, 4)
            group = jnp.maximum(unit, 0) // 4
            block = group // 2
            planes = (
                wrap(z + group + 1, PLANES),
                wrap(z - jnp.where(group == 7, 0, group + 1), PLANES),
            )

            @pl.when((unit >= 0) & (unit < 32) & (lax.rem(unit + 64, 8) == 0))
            def _():
                landed(rows.at[0, block], twin_recv.at[block])

            @pl.when((unit >= 0) & (unit < 32) & (quarter == 0))
            def _():
                for h, plane in enumerate(planes):
                    values = cols[pl.ds(plane * SUBS, SUBS)].reshape(SUBS * DEEP, WIDTH)
                    high, low = split(values)
                    cut[0, h * 128 : (h + 1) * 128, :] = high
                    cut[1, h * 128 : (h + 1) * 128, :] = low

            @pl.when((unit >= 0) & (unit < 32))
            def _():
                half = quarter // 2
                start = pl.multiple_of(lax.rem(quarter, 2) * 256, 256)
                slot = lax.rem(group, 2) * 2
                left = jnp.concatenate(
                    [
                        rows[half, block, :, :, slot + h, :, pl.ds(start, 256)].reshape(
                            SUBS * DEEP, 256
                        )
                        for h in range(2)
                    ],
                    axis=0,
                )
                high, low = split(left)
                place = pl.ds(pl.multiple_of(quarter * 256, 256), 256)
                out[place, :] += (
                    over_pairs(high, cut[0]) + over_pairs(high, cut[1]) + over_pairs(low, cut[0])
                )

    landed(outbox.at[pl.ds(0, PANELS - 1)], box_send)
    for side in range(2):
        landed(cols.at[pl.ds(0, STEPS)], ring_send.at[side])
    landed(row_box.at[pl.ds(0, PLANES - 1)], row_send)
    landed(swap_box, swap_send)

    landed(rows.at[0, 0, pl.ds(0, 3)], first_send)
    landed(rows.at[0, pl.ds(0, 3)], second_send)
    landed(rows.at[0], twin_send)


def per_device(
    pair_elements, valence_index, conduction_index, valence_energy, conduction_energy, chi_in
):
    return pl.pallas_call(
        kernel,
        out_shape=jax.ShapeDtypeStruct(chi_in.shape, jnp.float32),
        in_specs=[pl.BlockSpec(memory_space=pltpu.HBM)] * 6,
        out_specs=pl.BlockSpec(memory_space=pltpu.VMEM),
        scratch_shapes=[
            pltpu.SMEM((PAIRS,), jnp.int32),
            pltpu.SMEM((PAIRS,), jnp.int32),
            pltpu.VMEM((valence_energy.size // 128, 128), jnp.float32),
            pltpu.VMEM((conduction_energy.size // 128, 128), jnp.float32),
            pltpu.VMEM(pair_elements.shape, jnp.float32),
            pltpu.VMEM((PANELS, PAIRS, WIDTH), jnp.float32),
            pltpu.VMEM((PANELS, PAIRS, WIDTH), jnp.float32),
            pltpu.VMEM((PLANES, 2, PAIRS, WIDTH), jnp.float32),
            pltpu.VMEM((PLANES, PAIRS, WIDTH), jnp.float32),
            pltpu.VMEM((PLANES * SUBS, DEEP, WIDTH), jnp.float32),
            pltpu.VMEM((2, BLOCKS, 4, 4, 4, 2 * PAIRS, WIDTH), jnp.float32),
            pltpu.VMEM((2, 256, WIDTH), jnp.bfloat16),
            pltpu.SemaphoreType.DMA,
            pltpu.SemaphoreType.DMA((4,)),
            pltpu.SemaphoreType.DMA((2,)),
            pltpu.SemaphoreType.DMA((2, STEPS)),
            *[pltpu.SemaphoreType.DMA, pltpu.SemaphoreType.DMA((BLOCKS,))] * 5,
            pltpu.SemaphoreType.DMA((6,)),
        ],
        compiler_params=pltpu.CompilerParams(
            collective_id=0, has_side_effects=True, vmem_limit_bytes=63 * 1024 * 1024
        ),
    )(
        valence_index,
        conduction_index,
        valence_energy.reshape(-1, 128),
        conduction_energy.reshape(-1, 128),
        pair_elements,
        chi_in,
    )


def solution(mesh):
    placed = (
        P(("grow", "gcol"), None),
        P(("grow", "gcol")),
        P(("grow", "gcol")),
        P(),
        P(),
        P("grow", "gcol"),
    )
    return jax.shard_map(
        per_device, mesh=mesh, in_specs=placed, out_specs=P("grow", "gcol"), check_vma=False
    )
```

```python
import jax
import jax.numpy as jnp
from jax import lax
from jax.experimental import pallas as pl
from jax.experimental.pallas import tpu as pltpu
from jax.sharding import PartitionSpec as P

MESH = pl.DeviceIdType.MESH
PLANES = 16
PANELS = 32
PAIRS = 4
WIDTH = 512
SUBS = 4
DEEP = PANELS * PAIRS // SUBS
STEPS = 4 * (PLANES // 2) - 2
BLOCKS = 4
SLOT = {**{d: 2 * d - 2 for d in range(1, 8)}, **{16 - d: 2 * d - 1 for d in range(1, 8)}, 8: 14, 0: 15}
SWAP_AT = (0, 2, 4, 6)
FIRST_AT, SECOND_AT, TWIN_AT = (1, 3, 5, 7), (5, 9, 13, 17), (12, 17, 21, 25)
START, LAST_BLOCK = 15, 27
LAST = 30


def wrap(value, size):
    return lax.rem(value + 4 * size, size)


def looked_up(table, index):
    place = lax.broadcasted_iota(jnp.int32, table.shape, 0) * 128 + lax.broadcasted_iota(
        jnp.int32, table.shape, 1
    )
    return jnp.sum(jnp.where(place == index, table, 0.0), axis=(0, 1), keepdims=True)


def split(value):
    high = value.astype(jnp.bfloat16)
    return high, (value - high.astype(jnp.float32)).astype(jnp.bfloat16)


def over_pairs(left, right):
    return lax.dot_general(
        left, right, (((0,), (0,)), ((), ())), preferred_element_type=jnp.float32
    )


def landed(ref, sem):
    pltpu.make_async_copy(ref, ref, sem).wait()


def kernel(
    valence_index_in, conduction_index_in, valence_in, conduction_in, elements_in, chi, result,
    valence_index, conduction_index, valence, conduction, elements,
    out, outbox, inbox, row_box, swap_box, cols, rows, cut,
    box_send, box_recv, ring_send, ring_recv, row_send, row_recv,
    swap_send, swap_recv,
    first_send, first_recv, second_send, second_recv, twin_send, twin_recv, in_sem, out_sem,
):
    z = lax.axis_index("grow")
    c = lax.axis_index("gcol")
    core, x, y = lax.rem(c, 2), lax.rem(c // 2, 4), c // 8
    twin = c + 1 - 2 * core
    ahead, behind = wrap(z + 1, PLANES), wrap(z - 1, PLANES)

    loads = [
        pltpu.make_async_copy(source, target, in_sem.at[i])
        for i, (source, target) in enumerate(
            (
                (valence_index_in, valence_index),
                (conduction_index_in, conduction_index),
                (valence_in, valence),
                (conduction_in, conduction),
                (elements_in, elements),
                (chi, out),
            )
        )
    ]
    for load in loads:
        load.start()

    barrier = pltpu.get_barrier_semaphore()

    @pl.loop(1, PANELS)
    def _(k):
        pl.semaphore_signal(
            barrier, inc=1, device_id={"gcol": wrap(c + k, PANELS)}, device_id_type=MESH
        )

    @pl.loop(1, PLANES)
    def _(k):
        pl.semaphore_signal(
            barrier, inc=1, device_id={"grow": wrap(z + k, PLANES)}, device_id_type=MESH
        )

    for load in loads[:5]:
        load.wait()
    pair = lax.broadcasted_iota(jnp.int32, (PAIRS, 1), 0)
    gaps = jnp.ones((PAIRS, 1), jnp.float32)
    for i in range(PAIRS):
        gap = looked_up(conduction[...], conduction_index[i]) - looked_up(
            valence[...], valence_index[i]
        )
        gaps = jnp.where(pair == i, gap, gaps)
    root_weights = jnp.sqrt(4.0 / gaps)
    for k in range(PANELS):
        outbox[k] = elements[:, k * WIDTH : (k + 1) * WIDTH] * root_weights

    first, second = jnp.where(core == 0, x, y), jnp.where(core == 0, y, x)

    def at(second_place, first_place):
        line = jnp.where(
            core == 0, second_place * 4 + first_place, first_place * 4 + second_place
        )
        return line * 2 + core

    pl.semaphore_wait(barrier, PANELS - 1 + PLANES - 1)

    for distance, slot in sorted(SLOT.items(), key=lambda item: item[1]):
        to = wrap(z - distance, PLANES)
        source = outbox.at[pl.ds(2 * to, 2)]
        if distance:
            pltpu.make_async_remote_copy(
                src_ref=source,
                dst_ref=row_box.at[slot],
                send_sem=row_send,
                recv_sem=row_recv.at[slot // 4],
                device_id={"grow": to},
                device_id_type=MESH,
            ).start()
        else:
            pltpu.make_async_copy(source, row_box.at[slot], row_recv.at[slot // 4]).start()

    by_row, by_column = (y * 4 + x) * 2 + core, (x * 4 + y) * 2 + core

    @pl.loop(1, PANELS)
    def _(k):
        to = wrap(c + k, PANELS)
        place = jnp.where(lax.rem(to, 2) == 0, by_row, by_column)
        pltpu.make_async_remote_copy(
            src_ref=outbox.at[to],
            dst_ref=inbox.at[place],
            send_sem=box_send,
            recv_sem=box_recv.at[place // 8],
            device_id={"gcol": to},
            device_id_type=MESH,
        ).start()

    own = jnp.where(core == 0, by_row, by_column)
    pltpu.make_async_copy(outbox.at[c], inbox.at[own], box_recv.at[own // 8]).start()

    def pass_on(side, slot, step):
        pltpu.make_async_remote_copy(
            src_ref=cols.at[slot],
            dst_ref=cols.at[slot],
            send_sem=ring_send.at[side],
            recv_sem=ring_recv.at[side, step],
            device_id={"grow": (ahead, behind)[side]},
            device_id_type=MESH,
        ).start()

    for j in range(SUBS):
        landed(inbox.at[pl.ds(8 * j, 8)], box_recv.at[j])
        for k in range(8):
            cols[z * SUBS + j, k * PAIRS : (k + 1) * PAIRS, :] = inbox[8 * j + k]
        pass_on(0, z * SUBS + j, j)
        pass_on(1, z * SUBS + j, (j + 2) % 4)

    loads[5].wait()

    @pl.loop(-SUBS, LAST + 1)
    def _(i):
        q = wrap(i, 4)
        step = (i + 64) // 4 - 15

        @pl.when((i >= 0) & (i < STEPS))
        def _():
            for side, sub, plane in (
                (0, q, wrap(z - step, PLANES)),
                (1, wrap(q + 2, 4), wrap(z + step, PLANES)),
            ):
                slot = plane * SUBS + sub
                landed(cols.at[slot], ring_recv.at[side, i])

                @pl.when(i + SUBS < STEPS)
                def _():
                    pass_on(side, slot, i + SUBS)

        for block in range(BLOCKS):

            @pl.when(i == SWAP_AT[block])
            def _():
                landed(row_box.at[pl.ds(4 * block, 4)], row_recv.at[block])
                pltpu.make_async_remote_copy(
                    src_ref=row_box.at[pl.ds(4 * block, 4), 1 - core],
                    dst_ref=swap_box.at[pl.ds(4 * block, 4)],
                    send_sem=swap_send,
                    recv_sem=swap_recv.at[block],
                    device_id={"gcol": twin},
                    device_id_type=MESH,
                ).start()

            @pl.when(i == FIRST_AT[block])
            def _():
                landed(swap_box.at[pl.ds(4 * block, 4)], swap_recv.at[block])
                for slot in range(4):
                    own = row_box[4 * block + slot, core]
                    other = swap_box[4 * block + slot]
                    rows[core, block, second, first, slot, :PAIRS, :] = jnp.where(
                        core == 0, own, other
                    )
                    rows[core, block, second, first, slot, PAIRS:, :] = jnp.where(
                        core == 0, other, own
                    )
                piece = rows.at[core, block, second, first]
                for k in range(1, 4):
                    pltpu.make_async_remote_copy(
                        src_ref=piece,
                        dst_ref=piece,
                        send_sem=first_send,
                        recv_sem=first_recv.at[block],
                        device_id={"gcol": at(second, wrap(first + k, 4))},
                        device_id_type=MESH,
                    ).start()

            @pl.when(i == SECOND_AT[block])
            def _():
                landed(rows.at[core, block, second, pl.ds(0, 3)], first_recv.at[block])
                piece = rows.at[core, block, second]
                for k in range(1, 4):
                    pltpu.make_async_remote_copy(
                        src_ref=piece,
                        dst_ref=piece,
                        send_sem=second_send,
                        recv_sem=second_recv.at[block],
                        device_id={"gcol": at(wrap(second + k, 4), first)},
                        device_id_type=MESH,
                    ).start()

            @pl.when(i == TWIN_AT[block])
            def _():
                landed(rows.at[core, block, pl.ds(0, 3)], second_recv.at[block])
                for k in range(4):
                    pltpu.make_async_remote_copy(
                        src_ref=rows.at[core, block, k],
                        dst_ref=rows.at[core, block, pl.ds(0, 4), k],
                        send_sem=twin_send,
                        recv_sem=twin_recv.at[block],
                        device_id={"gcol": twin},
                        device_id_type=MESH,
                    ).start()

        def prepare(planes):
            for h, plane in enumerate(planes):
                values = cols[pl.ds(plane * SUBS, SUBS)].reshape(SUBS * DEEP, WIDTH)
                high, low = split(values)
                cut[0, h * 128 : (h + 1) * 128, :] = high
                cut[1, h * 128 : (h + 1) * 128, :] = low

        def multiply(block, quarter, slots):
            half = quarter // 2
            start = pl.multiple_of(lax.rem(quarter, 2) * 256, 256)
            left = jnp.concatenate(
                [
                    rows[half, block, :, :, slot, :, pl.ds(start, 256)].reshape(SUBS * DEEP, 256)
                    for slot in slots
                ],
                axis=0,
            )
            high, low = split(left)
            deep = len(slots) * 128
            place = pl.ds(pl.multiple_of(quarter * 256, 256), 256)
            out[place, :] += (
                over_pairs(high, cut[0, :deep])
                + over_pairs(high, cut[1, :deep])
                + over_pairs(low, cut[0, :deep])
            )
            return place

        @pl.when((i >= START) & (i < LAST_BLOCK))
        def _():
            block = (i - START) // 4
            quarter = lax.rem(i - START, 4)

            @pl.when(quarter == 0)
            def _():
                landed(rows.at[0, block], twin_recv.at[block])
                near = 2 * block + 1
                prepare([wrap(z + d, PLANES) for d in (near, -near, near + 1, -near - 1)])

            multiply(block, quarter, range(4))

        @pl.when(i == LAST_BLOCK)
        def _():
            landed(rows.at[0, BLOCKS - 1], twin_recv.at[BLOCKS - 1])

        @pl.when(i >= LAST_BLOCK)
        def _():
            last = (i - LAST_BLOCK) // 2

            @pl.loop(0, 2)
            def _(turn):
                quarter = lax.rem(i - LAST_BLOCK, 2) * 2 + turn

                @pl.when(quarter == 0)
                def _():
                    prepare([wrap(z + 7 + last, PLANES), wrap(z - jnp.where(last == 1, 0, 7), PLANES)])

                place = multiply(BLOCKS - 1, quarter, (2 * last, 2 * last + 1))

                @pl.when(last == 1)
                def _():
                    pltpu.make_async_copy(out.at[place], result.at[place], out_sem).start()

    landed(outbox.at[pl.ds(0, PANELS - 1)], box_send)
    for side in range(2):
        landed(cols.at[pl.ds(0, STEPS)], ring_send.at[side])
    landed(row_box.at[pl.ds(0, PLANES - 1)], row_send)
    landed(swap_box, swap_send)

    landed(rows.at[0, 0, pl.ds(0, 3)], first_send)
    landed(rows.at[0, pl.ds(0, 3)], second_send)
    landed(rows.at[0], twin_send)
    pltpu.make_async_copy(out, result, out_sem).wait()


def per_device(
    pair_elements, valence_index, conduction_index, valence_energy, conduction_energy, chi_in
):
    return pl.pallas_call(
        kernel,
        out_shape=jax.ShapeDtypeStruct(chi_in.shape, jnp.float32),
        in_specs=[pl.BlockSpec(memory_space=pltpu.HBM)] * 6,
        out_specs=pl.BlockSpec(memory_space=pltpu.HBM),
        scratch_shapes=[
            pltpu.SMEM((PAIRS,), jnp.int32),
            pltpu.SMEM((PAIRS,), jnp.int32),
            pltpu.VMEM((valence_energy.size // 128, 128), jnp.float32),
            pltpu.VMEM((conduction_energy.size // 128, 128), jnp.float32),
            pltpu.VMEM(pair_elements.shape, jnp.float32),
            pltpu.VMEM(chi_in.shape, jnp.float32),
            pltpu.VMEM((PANELS, PAIRS, WIDTH), jnp.float32),
            pltpu.VMEM((PANELS, PAIRS, WIDTH), jnp.float32),
            pltpu.VMEM((PLANES, 2, PAIRS, WIDTH), jnp.float32),
            pltpu.VMEM((PLANES, PAIRS, WIDTH), jnp.float32),
            pltpu.VMEM((PLANES * SUBS, DEEP, WIDTH), jnp.float32),
            pltpu.VMEM((2, BLOCKS, 4, 4, 4, 2 * PAIRS, WIDTH), jnp.float32),
            pltpu.VMEM((2, 512, WIDTH), jnp.bfloat16),
            pltpu.SemaphoreType.DMA,
            pltpu.SemaphoreType.DMA((4,)),
            pltpu.SemaphoreType.DMA((2,)),
            pltpu.SemaphoreType.DMA((2, STEPS)),
            *[pltpu.SemaphoreType.DMA, pltpu.SemaphoreType.DMA((BLOCKS,))] * 5,
            pltpu.SemaphoreType.DMA((6,)),
            pltpu.SemaphoreType.DMA,
        ],
        compiler_params=pltpu.CompilerParams(
            collective_id=0, has_side_effects=True, vmem_limit_bytes=63 * 1024 * 1024
        ),
    )(
        valence_index,
        conduction_index,
        valence_energy.reshape(-1, 128),
        conduction_energy.reshape(-1, 128),
        pair_elements,
        chi_in,
    )


def solution(mesh):
    placed = (
        P(("grow", "gcol"), None),
        P(("grow", "gcol")),
        P(("grow", "gcol")),
        P(),
        P(),
        P("grow", "gcol"),
    )
    return jax.shard_map(
        per_device, mesh=mesh, in_specs=placed, out_specs=P("grow", "gcol"), check_vma=False
    )
```

```python
import jax
import jax.numpy as jnp
from jax import lax
from jax.experimental import pallas as pl
from jax.experimental.pallas import tpu as pltpu
from jax.sharding import PartitionSpec as P

MESH = pl.DeviceIdType.MESH
PLANES = 16
PANELS = 32
PAIRS = 4
WIDTH = 512
SUBS = 4
DEEP = PANELS * PAIRS // SUBS
STEPS = 4 * (PLANES // 2) - 2
BLOCKS = 4
SLOT = {**{d: 2 * d - 2 for d in range(1, 8)}, **{16 - d: 2 * d - 1 for d in range(1, 8)}, 8: 14, 0: 15}
SWAP_AT = (0, 2, 4, 6)
FIRST_AT, SECOND_AT, TWIN_AT = (1, 3, 5, 7), (6, 10, 14, 18), (12, 17, 21, 25)
START, LAST_BLOCK = 15, 27
LAST = 30


def wrap(value, size):
    return lax.rem(value + 4 * size, size)


def looked_up(table, index):
    place = lax.broadcasted_iota(jnp.int32, table.shape, 0) * 128 + lax.broadcasted_iota(
        jnp.int32, table.shape, 1
    )
    return jnp.sum(jnp.where(place == index, table, 0.0), axis=(0, 1), keepdims=True)


def split(value):
    high = value.astype(jnp.bfloat16)
    return high, (value - high.astype(jnp.float32)).astype(jnp.bfloat16)


def over_pairs(left, right):
    return lax.dot_general(
        left, right, (((0,), (0,)), ((), ())), preferred_element_type=jnp.float32
    )


def landed(ref, sem):
    pltpu.make_async_copy(ref, ref, sem).wait()


def kernel(
    valence_index_in, conduction_index_in, valence_in, conduction_in, elements_in, chi, result,
    valence_index, conduction_index, valence, conduction, elements,
    out, outbox, inbox, row_box, swap_box, cols, rows, cut,
    box_send, box_recv, ring_send, ring_recv, row_send, row_recv,
    swap_send, swap_recv,
    first_send, first_recv, second_send, second_recv, twin_send, twin_recv, in_sem, out_sem,
):
    z = lax.axis_index("grow")
    c = lax.axis_index("gcol")
    core, x, y = lax.rem(c, 2), lax.rem(c // 2, 4), c // 8
    twin = c + 1 - 2 * core
    ahead, behind = wrap(z + 1, PLANES), wrap(z - 1, PLANES)

    loads = [
        pltpu.make_async_copy(source, target, in_sem.at[i])
        for i, (source, target) in enumerate(
            (
                (valence_index_in, valence_index),
                (conduction_index_in, conduction_index),
                (valence_in, valence),
                (conduction_in, conduction),
                (elements_in, elements),
                (chi, out),
            )
        )
    ]
    for load in loads:
        load.start()

    barrier = pltpu.get_barrier_semaphore()

    @pl.loop(1, PANELS)
    def _(k):
        pl.semaphore_signal(
            barrier, inc=1, device_id={"gcol": wrap(c + k, PANELS)}, device_id_type=MESH
        )

    @pl.loop(1, PLANES)
    def _(k):
        pl.semaphore_signal(
            barrier, inc=1, device_id={"grow": wrap(z + k, PLANES)}, device_id_type=MESH
        )

    for load in loads[:5]:
        load.wait()
    pair = lax.broadcasted_iota(jnp.int32, (PAIRS, 1), 0)
    gaps = jnp.ones((PAIRS, 1), jnp.float32)
    for i in range(PAIRS):
        gap = looked_up(conduction[...], conduction_index[i]) - looked_up(
            valence[...], valence_index[i]
        )
        gaps = jnp.where(pair == i, gap, gaps)
    root_weights = jnp.sqrt(4.0 / gaps)
    for k in range(PANELS):
        outbox[k] = elements[:, k * WIDTH : (k + 1) * WIDTH] * root_weights

    first, second = jnp.where(core == 0, x, y), jnp.where(core == 0, y, x)

    def at(second_place, first_place):
        line = jnp.where(
            core == 0, second_place * 4 + first_place, first_place * 4 + second_place
        )
        return line * 2 + core

    pl.semaphore_wait(barrier, PANELS - 1 + PLANES - 1)

    for distance, slot in sorted(SLOT.items(), key=lambda item: item[1]):
        to = wrap(z - distance, PLANES)
        source = outbox.at[pl.ds(2 * to, 2)]
        if distance:
            pltpu.make_async_remote_copy(
                src_ref=source,
                dst_ref=row_box.at[slot],
                send_sem=row_send,
                recv_sem=row_recv.at[slot // 4],
                device_id={"grow": to},
                device_id_type=MESH,
            ).start()
        else:
            pltpu.make_async_copy(source, row_box.at[slot], row_recv.at[slot // 4]).start()

    by_row, by_column = (y * 4 + x) * 2 + core, (x * 4 + y) * 2 + core

    @pl.loop(1, PANELS)
    def _(k):
        to = wrap(c + k, PANELS)
        place = jnp.where(lax.rem(to, 2) == 0, by_row, by_column)
        pltpu.make_async_remote_copy(
            src_ref=outbox.at[to],
            dst_ref=inbox.at[place],
            send_sem=box_send,
            recv_sem=box_recv.at[place // 8],
            device_id={"gcol": to},
            device_id_type=MESH,
        ).start()

    own = jnp.where(core == 0, by_row, by_column)
    pltpu.make_async_copy(outbox.at[c], inbox.at[own], box_recv.at[own // 8]).start()

    def pass_on(side, slot, step):
        pltpu.make_async_remote_copy(
            src_ref=cols.at[slot],
            dst_ref=cols.at[slot],
            send_sem=ring_send.at[side],
            recv_sem=ring_recv.at[side, step],
            device_id={"grow": (ahead, behind)[side]},
            device_id_type=MESH,
        ).start()

    for j in range(SUBS):
        landed(inbox.at[pl.ds(8 * j, 8)], box_recv.at[j])
        for k in range(8):
            cols[z * SUBS + j, k * PAIRS : (k + 1) * PAIRS, :] = inbox[8 * j + k]
        pass_on(0, z * SUBS + j, j)
        pass_on(1, z * SUBS + j, (j + 2) % 4)

    loads[5].wait()

    @pl.loop(-SUBS, LAST + 1)
    def _(i):
        q = wrap(i, 4)
        step = (i + 64) // 4 - 15

        @pl.when((i >= 0) & (i < STEPS))
        def _():
            for side, sub, plane in (
                (0, q, wrap(z - step, PLANES)),
                (1, wrap(q + 2, 4), wrap(z + step, PLANES)),
            ):
                slot = plane * SUBS + sub
                landed(cols.at[slot], ring_recv.at[side, i])

                @pl.when(i + SUBS < STEPS)
                def _():
                    pass_on(side, slot, i + SUBS)

        for block in range(BLOCKS):

            @pl.when(i == SWAP_AT[block])
            def _():
                landed(row_box.at[pl.ds(4 * block, 4)], row_recv.at[block])
                pltpu.make_async_remote_copy(
                    src_ref=row_box.at[pl.ds(4 * block, 4), 1 - core],
                    dst_ref=swap_box.at[pl.ds(4 * block, 4)],
                    send_sem=swap_send,
                    recv_sem=swap_recv.at[block],
                    device_id={"gcol": twin},
                    device_id_type=MESH,
                ).start()

            @pl.when(i == FIRST_AT[block])
            def _():
                landed(swap_box.at[pl.ds(4 * block, 4)], swap_recv.at[block])
                for slot in range(4):
                    own = row_box[4 * block + slot, core]
                    other = swap_box[4 * block + slot]
                    rows[core, block, second, first, slot, :PAIRS, :] = jnp.where(
                        core == 0, own, other
                    )
                    rows[core, block, second, first, slot, PAIRS:, :] = jnp.where(
                        core == 0, other, own
                    )
                piece = rows.at[core, block, second, first]
                for k in range(1, 4):
                    pltpu.make_async_remote_copy(
                        src_ref=piece,
                        dst_ref=piece,
                        send_sem=first_send,
                        recv_sem=first_recv.at[block],
                        device_id={"gcol": at(second, wrap(first + k, 4))},
                        device_id_type=MESH,
                    ).start()

            @pl.when(i == SECOND_AT[block])
            def _():
                landed(rows.at[core, block, second, pl.ds(0, 3)], first_recv.at[block])
                piece = rows.at[core, block, second]
                for k in range(1, 4):
                    pltpu.make_async_remote_copy(
                        src_ref=piece,
                        dst_ref=piece,
                        send_sem=second_send,
                        recv_sem=second_recv.at[block],
                        device_id={"gcol": at(wrap(second + k, 4), first)},
                        device_id_type=MESH,
                    ).start()

            @pl.when(i == TWIN_AT[block])
            def _():
                landed(rows.at[core, block, pl.ds(0, 3)], second_recv.at[block])
                for k in range(4):
                    pltpu.make_async_remote_copy(
                        src_ref=rows.at[core, block, k],
                        dst_ref=rows.at[core, block, pl.ds(0, 4), k],
                        send_sem=twin_send,
                        recv_sem=twin_recv.at[block],
                        device_id={"gcol": twin},
                        device_id_type=MESH,
                    ).start()

        def prepare(planes):
            for h, plane in enumerate(planes):
                values = cols[pl.ds(plane * SUBS, SUBS)].reshape(SUBS * DEEP, WIDTH)
                high, low = split(values)
                cut[0, h * 128 : (h + 1) * 128, :] = high
                cut[1, h * 128 : (h + 1) * 128, :] = low

        def multiply(block, quarter, slots):
            half = quarter // 2
            start = pl.multiple_of(lax.rem(quarter, 2) * 256, 256)
            left = jnp.concatenate(
                [
                    rows[half, block, :, :, slot, :, pl.ds(start, 256)].reshape(SUBS * DEEP, 256)
                    for slot in slots
                ],
                axis=0,
            )
            high, low = split(left)
            deep = len(slots) * 128
            place = pl.ds(pl.multiple_of(quarter * 256, 256), 256)
            out[place, :] += (
                over_pairs(high, cut[0, :deep])
                + over_pairs(high, cut[1, :deep])
                + over_pairs(low, cut[0, :deep])
            )
            return place

        @pl.when((i >= START) & (i < LAST_BLOCK))
        def _():
            block = (i - START) // 4
            quarter = lax.rem(i - START, 4)

            @pl.when(quarter == 0)
            def _():
                landed(rows.at[0, block], twin_recv.at[block])
                near = 2 * block + 1
                prepare([wrap(z + d, PLANES) for d in (near, -near, near + 1, -near - 1)])

            multiply(block, quarter, range(4))

        @pl.when(i == LAST_BLOCK)
        def _():
            landed(rows.at[0, BLOCKS - 1], twin_recv.at[BLOCKS - 1])

        @pl.when(i >= LAST_BLOCK)
        def _():
            last = (i - LAST_BLOCK) // 2

            @pl.loop(0, 2)
            def _(turn):
                quarter = lax.rem(i - LAST_BLOCK, 2) * 2 + turn

                @pl.when(quarter == 0)
                def _():
                    prepare([wrap(z + 7 + last, PLANES), wrap(z - jnp.where(last == 1, 0, 7), PLANES)])

                place = multiply(BLOCKS - 1, quarter, (2 * last, 2 * last + 1))

                @pl.when(last == 1)
                def _():
                    pltpu.make_async_copy(out.at[place], result.at[place], out_sem).start()

    landed(outbox.at[pl.ds(0, PANELS - 1)], box_send)
    for side in range(2):
        landed(cols.at[pl.ds(0, STEPS)], ring_send.at[side])
    landed(row_box.at[pl.ds(0, PLANES - 1)], row_send)
    landed(swap_box, swap_send)

    landed(rows.at[0, 0, pl.ds(0, 3)], first_send)
    landed(rows.at[0, pl.ds(0, 3)], second_send)
    landed(rows.at[0], twin_send)
    pltpu.make_async_copy(out, result, out_sem).wait()


def per_device(
    pair_elements, valence_index, conduction_index, valence_energy, conduction_energy, chi_in
):
    return pl.pallas_call(
        kernel,
        out_shape=jax.ShapeDtypeStruct(chi_in.shape, jnp.float32),
        in_specs=[pl.BlockSpec(memory_space=pltpu.HBM)] * 6,
        out_specs=pl.BlockSpec(memory_space=pltpu.HBM),
        scratch_shapes=[
            pltpu.SMEM((PAIRS,), jnp.int32),
            pltpu.SMEM((PAIRS,), jnp.int32),
            pltpu.VMEM((valence_energy.size // 128, 128), jnp.float32),
            pltpu.VMEM((conduction_energy.size // 128, 128), jnp.float32),
            pltpu.VMEM(pair_elements.shape, jnp.float32),
            pltpu.VMEM(chi_in.shape, jnp.float32),
            pltpu.VMEM((PANELS, PAIRS, WIDTH), jnp.float32),
            pltpu.VMEM((PANELS, PAIRS, WIDTH), jnp.float32),
            pltpu.VMEM((PLANES, 2, PAIRS, WIDTH), jnp.float32),
            pltpu.VMEM((PLANES, PAIRS, WIDTH), jnp.float32),
            pltpu.VMEM((PLANES * SUBS, DEEP, WIDTH), jnp.float32),
            pltpu.VMEM((2, BLOCKS, 4, 4, 4, 2 * PAIRS, WIDTH), jnp.float32),
            pltpu.VMEM((2, 512, WIDTH), jnp.bfloat16),
            pltpu.SemaphoreType.DMA,
            pltpu.SemaphoreType.DMA((4,)),
            pltpu.SemaphoreType.DMA((2,)),
            pltpu.SemaphoreType.DMA((2, STEPS)),
            *[pltpu.SemaphoreType.DMA, pltpu.SemaphoreType.DMA((BLOCKS,))] * 5,
            pltpu.SemaphoreType.DMA((6,)),
            pltpu.SemaphoreType.DMA,
        ],
        compiler_params=pltpu.CompilerParams(
            collective_id=0, has_side_effects=True, vmem_limit_bytes=63 * 1024 * 1024
        ),
    )(
        valence_index,
        conduction_index,
        valence_energy.reshape(-1, 128),
        conduction_energy.reshape(-1, 128),
        pair_elements,
        chi_in,
    )


def solution(mesh):
    placed = (
        P(("grow", "gcol"), None),
        P(("grow", "gcol")),
        P(("grow", "gcol")),
        P(),
        P(),
        P("grow", "gcol"),
    )
    return jax.shard_map(
        per_device, mesh=mesh, in_specs=placed, out_specs=P("grow", "gcol"), check_vma=False
    )
```
